32 devices in a mesh: outer: 16 (over z, y, core), inner: 2 (over x).
Axes of the slice: x: 2, y: 2, z: 4, core: 2. Of those that a mesh axis runs over, the one named last changes fastest.
Arguments:
- layer_input: bfloat16 [4096, 8192], P(('outer', 'inner')), may hold values from -6 to 6
- queries: bfloat16 [4096, 4096], P(('outer', 'inner')), may hold values from -8 to 8
- key_states: bfloat16 [4096, 512], P(('outer', 'inner')), may hold values from -8 to 8
- output_grad: bfloat16 [4096, 4096], P(('outer', 'inner')), may hold values from -24 to 24
- value_weight: bfloat16 [8192, 512], P('inner'), may hold values from -0.0625 to 0.0625
- value_scales: float32 [8192, 2], P('inner'), may hold values from 0.5 to 2
Outputs:
- query_grad: bfloat16 [4096, 4096], P(('outer', 'inner'))
- key_grad: bfloat16 [4096, 512], P(('outer', 'inner'))
- weight_grad: float32 [8192, 512], P(('outer', 'inner'))
The draws below stay inside these ranges and needn't reach their ends.
All inputs are finite; a program needn't handle non-finite values.
Results may differ from the reference program's by a relative error of at most 0.034.
Values may be sent and summed in bfloat16 or wider, within the bound.
A program may use at most 192 MiB of HBM per device.

```python
import math
import jax
import jax.numpy as jnp
from jax import lax

MODEL_WIDTH = 8192
QUERY_HEADS = 32
KV_HEADS = 4
HEAD_DIM = 128
QUANT_BLOCK = 256
TOK_DEV = 128
GROUP_SIZE = 8
QUERY_WIDTH = 4096
KV_WIDTH = 512
TOKENS = 4096


def draw_queries(key, part):
    key = jax.random.fold_in(key, 1)
    array_shape = (TOKENS, QUERY_HEADS * HEAD_DIM)
    values = jnp.clip(jax.random.normal(key, array_shape, jnp.float32), -6.0, 6.0)
    return values.astype(jnp.bfloat16)


def draw_key_states(key, part):
    key = jax.random.fold_in(key, 3)
    array_shape = (TOKENS, KV_HEADS * HEAD_DIM)
    values = jnp.clip(jax.random.normal(key, array_shape, jnp.float32), -6.0, 6.0)
    return values.astype(jnp.bfloat16)


def strengthened(drawn, key, source, target, parts, factor):
    def block_of(axis_at):
        return (jnp.arange(drawn.shape[axis_at]) // (drawn.shape[axis_at] // parts)).reshape((-1,) + (1,) * (drawn.ndim - 1 - axis_at))

    one_side = jax.random.permutation(key, parts)[block_of(target)]
    second = (block_of(target) + parts // 2) % parts
    return jnp.where((block_of(source) == one_side) | (block_of(source) == second), factor * drawn, drawn)


def level_of(stream_key, dims, shards, least, high):
    gain, own = 1.0, jax.random.fold_in(stream_key, 6)
    for axis_at, shards_of in shards:
        draws = jnp.exp(jax.random.uniform(jax.random.fold_in(own, axis_at), (shards_of,), jnp.float32, least / len(shards), high / len(shards)))
        gain = gain * jnp.repeat(draws, dims[axis_at] // shards_of).reshape([-1 if axis == axis_at else 1 for axis in range(len(dims))])
    return gain


def noise(key, extent, spread, most, shards=(), held_as=jnp.bfloat16):
    array = spread * jax.random.normal(key, extent, jnp.float32)
    if shards:
        array = array * level_of(key, extent, shards, -0.22, 0.18)
    return jnp.clip(array, -most, most).astype(held_as)


def noise_with(stream_key, shape, scale, most, shards, heavy, kind=jnp.bfloat16):
    entries = scale * jax.random.normal(stream_key, shape, jnp.float32)
    if shards:
        entries = entries * level_of(stream_key, shape, shards, -0.22, 0.18)
    return jnp.clip(strengthened(entries, jax.random.fold_in(stream_key, 3), *heavy), -most, most).astype(kind)


def setup_inputs(seed: int = 0) -> dict:
    streams_of = jax.random.split(jax.random.key(seed), 7)
    return {
        "layer_input": noise_with(streams_of[0], (TOKENS, MODEL_WIDTH), 1.0, 6.0, ((0, 32),), (0, 1, 32, 2.75)),
        "queries": draw_queries(jax.random.fold_in(streams_of[6], 71), 0),
        "key_states": draw_key_states(jax.random.fold_in(streams_of[6], 71), 0),
        "output_grad": noise(streams_of[3], (TOKENS, QUERY_WIDTH), 4.0, 24.0, ((0, 32),)),
        "value_weight": noise(streams_of[4], (MODEL_WIDTH, KV_WIDTH), MODEL_WIDTH ** -0.5, 0.0625, ((0, 2),)),
        "value_scales": jnp.clip(jnp.exp(math.log(2.0) - 1.3862944 * jax.random.uniform(streams_of[5], (MODEL_WIDTH, KV_WIDTH // QUANT_BLOCK), jnp.float32) ** level_of(streams_of[5], (MODEL_WIDTH, KV_WIDTH // QUANT_BLOCK), ((0, 2),), -0.2, 0.2)), 0.5, 2.0),
    }


clip_ratio = 1.5

def dequantize(quant_values, quant_scales):
    leading = quant_values.shape[:-1]
    blocks = quant_values.astype(jnp.float32).reshape(leading + (quant_scales.shape[-1], -1))
    return (blocks * quant_scales[..., None]).reshape(leading + (-1,))

def quantize(gradient):
    leading = gradient.shape[:-1]
    blocks = gradient.reshape(leading + (-1, QUANT_BLOCK))
    block_scale = clip_ratio * jnp.sqrt(lax.optimization_barrier(jnp.mean(blocks * blocks, axis=-1)) + 1e-06)
    scaled = jnp.clip(blocks / block_scale[..., None], -1.0, 1.0)
    quant = scaled.astype(jnp.bfloat16).reshape(gradient.shape)
    return (quant, block_scale)

def attend_backward(queries, key_states, value_rows, output_grad):
    count = queries.shape[0]
    query_heads = queries.astype(jnp.float32).reshape(count, KV_HEADS, GROUP_SIZE, HEAD_DIM)
    key_heads = key_states.astype(jnp.float32).reshape(count, KV_HEADS, HEAD_DIM)
    value_heads = value_rows.astype(jnp.float32).reshape(count, KV_HEADS, HEAD_DIM)
    grad_heads = output_grad.astype(jnp.float32).reshape(count, KV_HEADS, GROUP_SIZE, HEAD_DIM)
    score_scale = HEAD_DIM ** (-0.5)
    scores = score_scale * jnp.einsum('tgek,sgk->gets', query_heads, key_heads)
    position = jnp.arange(count)
    causal = position[:, None] >= position[None, :]
    scores = jnp.where(causal, scores, -jnp.inf)
    row_peak = lax.optimization_barrier(jnp.max(scores, axis=-1, keepdims=True))
    exp_scores = jnp.exp(scores - row_peak)
    probs = exp_scores / lax.optimization_barrier(jnp.sum(exp_scores, axis=-1, keepdims=True))
    probs_low = lax.optimization_barrier(probs.astype(jnp.bfloat16)).astype(jnp.float32)
    value_grad = jnp.einsum('gets,tgek->sgk', probs_low, grad_heads).astype(jnp.bfloat16)
    prob_grad = jnp.einsum('tgek,sgk->gets', grad_heads, value_heads)
    row_delta = lax.optimization_barrier(jnp.sum(probs * prob_grad, axis=-1, keepdims=True))
    score_grad = lax.optimization_barrier((probs * (prob_grad - row_delta)).astype(jnp.bfloat16)).astype(jnp.float32)
    query_grad = (score_scale * jnp.einsum('gets,sgk->tgek', score_grad, key_heads)).astype(jnp.bfloat16)
    key_grad = (score_scale * jnp.einsum('gets,tgek->sgk', score_grad, query_heads)).astype(jnp.bfloat16)
    return (query_grad.reshape(count, -1), key_grad.reshape(count, -1), value_grad.reshape(count, -1))

def reference(layer_input, queries, key_states, output_grad, value_weight, value_scales):
    weight = dequantize(value_weight, value_scales).astype(jnp.bfloat16)
    sequences = layer_input.shape[0] // TOK_DEV

    def one_sequence(running, index):
        offset = index * TOK_DEV
        inputs_n = lax.dynamic_slice_in_dim(layer_input, offset, TOK_DEV, 0)
        queries_n = lax.dynamic_slice_in_dim(queries, offset, TOK_DEV, 0)
        keys_n = lax.dynamic_slice_in_dim(key_states, offset, TOK_DEV, 0)
        grads_n = lax.dynamic_slice_in_dim(output_grad, offset, TOK_DEV, 0)
        value_rows = jnp.dot(inputs_n, weight, preferred_element_type=jnp.float32).astype(jnp.bfloat16)
        query_grad, key_grad, value_grad = attend_backward(queries_n, keys_n, value_rows, grads_n)
        gradient = jnp.dot(inputs_n.T, value_grad, preferred_element_type=jnp.float32)
        quant, block_scale = quantize(gradient)
        return (running + dequantize(quant, block_scale), (query_grad, key_grad))
    start_grad = jnp.zeros((MODEL_WIDTH, KV_WIDTH), jnp.float32)
    weight_grad, (query_grad, key_grad) = lax.scan(one_sequence, start_grad, jnp.arange(sequences, dtype=jnp.int32))
    return (query_grad.reshape(-1, QUERY_WIDTH), key_grad.reshape(-1, KV_WIDTH), weight_grad)
```

```python
import functools
import jax
import jax.numpy as jnp
from jax import lax
from jax.experimental import pallas as pl
from jax.experimental.pallas import tpu as pltpu
from jax.sharding import PartitionSpec as P

HEAD_DIM = 128
QUANT_BLOCK = 256
CLIP_RATIO = 1.5
Z_SPLIT = 4
F32 = jnp.float32
BF16 = jnp.bfloat16


def dot(a, b, ca=1, cb=0):
    return lax.dot_general(a, b, (((ca,), (cb,)), ((), ())), preferred_element_type=F32)


def body(dims, li, q_hbm, k_hbm, g_hbm, w_hbm, sc_ref, dq_out, dk_out, dw_out,
         q, k, g, w, xbuf, tbuf, vgbuf, probs, vals, vsend, vrecv, acc, pbuf, rbuf,
         loc_sem, own_sem, xs_sem, xr_sem, fs_sem, fr_sem, gxs_sem, gxr_sem, gfs_sem, gfr_sem,
         vs_sem, vr_sem, zs_sem, zr_sem):
    outer, inner, lo, runs, oc, kv_heads, group = dims
    o = lax.axis_index("outer")
    x = lax.axis_index("inner")
    z = o // lo
    l = o % lo
    part = outer * oc
    per = Z_SPLIT // runs
    width = per * oc
    count = q.shape[0]
    scale = HEAD_DIM ** -0.5

    def col(e, r):
        return pl.multiple_of(r * (outer // runs) * oc + ((l + e) % lo) * width, 128)

    def xdev(e):
        return (o, (x + e) % inner)

    def ldev(e):
        return (z * lo + (l + e) % lo, x)

    def remote(src, dst, ss, rs, dev):
        return pltpu.make_async_remote_copy(
            src_ref=src, dst_ref=dst, send_sem=ss, recv_sem=rs, device_id=dev,
            device_id_type=pl.DeviceIdType.MESH)

    q_cp = pltpu.make_async_copy(q_hbm, q, loc_sem.at[0])
    k_cp = pltpu.make_async_copy(k_hbm, k, loc_sem.at[1])
    g_cp = pltpu.make_async_copy(g_hbm, g, loc_sem.at[2])
    w_cp = pltpu.make_async_copy(w_hbm, w, loc_sem.at[3])
    order = [(r, e) for r in range(runs) for e in list(range(1, lo)) + [0]]
    order = [(r, e) for r in range(runs) for e in [lo // 2 + i for i in range(lo - lo // 2)]
             + [i for i in range(1, lo // 2)] + [0]] if lo > 1 else order

    def x_copy(ex, e, r):
        cols = pl.multiple_of(((x + ex) % inner) * part + col(e, r), 128)
        return remote(li.at[:, pl.ds(cols, width)], xbuf.at[inner - ex, e, r],
                      xs_sem.at[ex, e, r], xr_sem.at[inner - ex, e, r], xdev(ex))

    def own_copy(e, r):
        cols = pl.multiple_of(x * part + col(e, r), 128)
        return pltpu.make_async_copy(li.at[:, pl.ds(cols, width)], xbuf.at[0, e, r], own_sem.at[e, r])

    def fwd_own(e, r):
        cols = pl.multiple_of(x * part + col(e, r), 128)
        return remote(li.at[:, pl.ds(cols, width)], tbuf.at[lo - e, 0, r],
                      fs_sem.at[e, 0, r], fr_sem.at[lo - e, 0, r], ldev(e))

    def fwd(s, e, r):
        return remote(xbuf.at[s, e, r], tbuf.at[lo - e, s, r],
                      fs_sem.at[e, s, r], fr_sem.at[lo - e, s, r], ldev(e))

    q_cp.start()
    k_cp.start()
    for r, e in order:
        for ex in range(1, inner):
            x_copy(ex, e, r).start()
        if e:
            fwd_own(e, r).start()
    g_cp.start()
    for r, e in order:
        own_copy(e, r).start()
    w_cp.start()

    q_cp.wait()
    k_cp.wait()
    g_cp.wait()
    span = group * HEAD_DIM

    def heads(ref, h):
        return jnp.concatenate(
            [ref[:, (h * group + e) * HEAD_DIM:(h * group + e + 1) * HEAD_DIM] for e in range(group)], axis=0)

    key_pos = lax.broadcasted_iota(jnp.int32, (count, group * count), 0)
    query_pos = lax.broadcasted_iota(jnp.int32, (count, group * count), 1) % count
    admitted = key_pos <= query_pos
    for h in range(kv_heads):
        keys = k[:, h * HEAD_DIM:(h + 1) * HEAD_DIM]
        st = dot(keys, heads(q, h), 1, 1)
        st = jnp.where(admitted, st, -1e30)
        ex = jnp.exp((st - jnp.max(st, axis=0, keepdims=True)) * scale)
        p = ex * (1.0 / jnp.sum(ex, axis=0, keepdims=True))
        probs[h] = p
        vg = dot(p.astype(BF16), heads(g, h))
        vgbuf[0, 0, h * HEAD_DIM:(h + 1) * HEAD_DIM, :] = vg.T.astype(BF16)

    def vg_x(ex):
        return remote(vgbuf.at[0, 0], vgbuf.at[0, inner - ex], gxs_sem.at[ex], gxr_sem.at[inner - ex], xdev(ex))

    def vg_f(e, s):
        return remote(vgbuf.at[0, s], vgbuf.at[lo - e, s], gfs_sem.at[e, s], gfr_sem.at[lo - e, s], ldev(e))

    for ex in range(1, inner):
        vg_x(ex).start()
    for e in range(1, lo):
        vg_f(e, 0).start()

    w_cp.wait()
    first = True
    for r, e in order:
        own_copy(e, r).wait()
        for s in range(1, inner):
            x_copy(inner - s, e, r).wait_recv()
            if e:
                fwd(s, e, r).start()
        start = col(e, r)
        for j in range(vals.shape[-1] // QUANT_BLOCK):
            block = slice(j * QUANT_BLOCK, (j + 1) * QUANT_BLOCK)
            row_scale = sc_ref[j:j + 1, pl.ds(start, width)]
            lhs = jnp.concatenate(
                [(xbuf[s, e, r].astype(F32) * row_scale).astype(BF16) for s in range(inner)], axis=0)
            add = dot(lhs, w[pl.ds(start, width), block]).reshape(inner, count, QUANT_BLOCK)
            if first:
                vals[:, :, block] = add
            else:
                vals[:, :, block] += add
        first = False

    def val_copy(ex):
        return remote(vsend.at[ex], vrecv.at[inner - ex], vs_sem.at[ex], vr_sem.at[inner - ex], xdev(ex))

    for ex in range(1, inner):
        vsend[ex] = vals[ex].astype(BF16)
        val_copy(ex).start()
    for s in range(1, inner):
        vg_x(inner - s).wait_recv()
        for e in range(1, lo):
            vg_f(e, s).start()

    tile = min(width, 256)

    def add_term(vg_of, data_of, r, fresh):
        def step(c, carry):
            at = pl.multiple_of(c * tile, 128)
            data = data_of(at)
            for j in range(acc.shape[1] // QUANT_BLOCK):
                rows = slice(j * QUANT_BLOCK, (j + 1) * QUANT_BLOCK)
                term = dot(vg_of(rows), data)
                mean = jnp.sum(term * term, axis=0, keepdims=True) * (1.0 / QUANT_BLOCK)
                bound = CLIP_RATIO * jnp.sqrt(mean + 1e-6)
                kept = jnp.minimum(jnp.maximum(term, -bound), bound)
                if fresh:
                    acc[r, rows, pl.ds(at, tile)] = kept
                else:
                    acc[r, rows, pl.ds(at, tile)] += kept
            return carry
        lax.fori_loop(0, width // tile, step, 0)

    def owner(r, j):
        index = x * outer + r * (outer // runs) + l * per + j
        return index // inner, index % inner

    def z_copy(r, j):
        oo, xx = owner(r, j)
        n = r * per + j
        return remote(pbuf.at[n], rbuf.at[z], zs_sem.at[n], zr_sem.at[z], (oo, xx))

    def is_me(r, j):
        oo, xx = owner(r, j)
        return jnp.logical_and(oo == o, xx == x)

    def terms(r):
        for s in range(inner):
            add_term(lambda rows, s=s: vgbuf[0, s, rows, :],
                     lambda at, s=s: xbuf[s, 0, r, :, pl.ds(at, tile)], r, s == 0)
        for s in range(inner):
            def from_peer(d, carry, s=s):
                pltpu.make_async_copy(tbuf.at[d, s, r], tbuf.at[d, s, r], fr_sem.at[d, s, r]).wait()
                if r == 0:
                    pltpu.make_async_copy(vgbuf.at[d, s], vgbuf.at[d, s], gfr_sem.at[d, s]).wait()
                add_term(lambda rows: vgbuf[d, s, rows, :],
                         lambda at: tbuf[d, s, r, :, pl.ds(at, tile)], r, False)
                return carry
            lax.fori_loop(1, lo, from_peer, 0)
        summed = acc[r].T.astype(BF16)
        for j in range(per):
            n = r * per + j
            pbuf[n] = summed[j * oc:(j + 1) * oc]

            @pl.when(jnp.logical_not(is_me(r, j)))
            def _():
                z_copy(r, j).start()

            @pl.when(is_me(r, j))
            def _():
                pltpu.make_async_copy(pbuf.at[n], rbuf.at[z], zr_sem.at[z]).start()

    for r in range(runs):
        terms(r)

    for s in range(1, inner):
        val_copy(inner - s).wait_recv()
    total = vals[0]
    for s in range(1, inner):
        total = total + vrecv[s].astype(F32)
    values = total.astype(BF16)
    for h in range(kv_heads):
        cols = slice(h * HEAD_DIM, (h + 1) * HEAD_DIM)
        keys = k[:, cols]
        dp = dot(values[:, cols], heads(g, h), 1, 1)
        p = probs[h]
        delta = jnp.sum(p * dp, axis=0, keepdims=True)
        ds = p * (dp - delta)
        dk_out[:, cols] = (dot(ds.astype(BF16), heads(q, h)) * scale).astype(BF16)
        dq = (dot(ds.T.astype(BF16), keys) * scale).astype(BF16)
        for e in range(group):
            dq_out[:, (h * group + e) * HEAD_DIM:(h * group + e + 1) * HEAD_DIM] = dq[e * count:(e + 1) * count]

    for n in range(Z_SPLIT):
        pltpu.make_async_copy(rbuf.at[n], rbuf.at[n], zr_sem.at[n]).wait()
    out = rbuf[0].astype(F32)
    for n in range(1, Z_SPLIT):
        out = out + rbuf[n].astype(F32)
    dw_out[...] = out

    for ex in range(1, inner):
        vg_x(ex).wait_send()
        val_copy(ex).wait_send()
        for r, e in order:
            x_copy(ex, e, r).wait_send()
    for e in range(1, lo):
        for s in range(inner):
            vg_f(e, s).wait_send()
            for r in range(runs):
                (fwd(s, e, r) if s else fwd_own(e, r)).wait_send()
    for r in range(runs):
        for j in range(per):
            @pl.when(jnp.logical_not(is_me(r, j)))
            def _():
                z_copy(r, j).wait_send()


def on_device(layer_input, queries, key_states, output_grad, value_weight, value_scales):
    outer = lax.axis_size("outer")
    inner = lax.axis_size("inner")
    lo = outer // Z_SPLIT
    count, model = layer_input.shape
    kv = key_states.shape[1]
    oc = model // (outer * inner)
    runs = 2 if (2 * oc) % 128 == 0 else 1
    per = Z_SPLIT // runs
    width = per * oc
    kv_heads = kv // HEAD_DIM
    group = queries.shape[1] // kv
    dims = (outer, inner, lo, runs, oc, kv_heads, group)
    dma = pltpu.SemaphoreType.DMA
    anyspace = pl.BlockSpec(memory_space=pl.ANY)
    vmem = pl.BlockSpec(memory_space=pltpu.VMEM)
    return pl.pallas_call(
        functools.partial(body, dims),
        out_shape=(
            jax.ShapeDtypeStruct(queries.shape, BF16),
            jax.ShapeDtypeStruct(key_states.shape, BF16),
            jax.ShapeDtypeStruct((oc, kv), F32),
        ),
        in_specs=[anyspace] * 5 + [vmem],
        out_specs=(vmem, vmem, vmem),
        scratch_shapes=[
            pltpu.VMEM(queries.shape, BF16),
            pltpu.VMEM(key_states.shape, BF16),
            pltpu.VMEM(output_grad.shape, BF16),
            pltpu.VMEM(value_weight.shape, BF16),
            pltpu.VMEM((inner, lo, runs, count, width), BF16),
            pltpu.VMEM((lo, inner, runs, count, width), BF16),
            pltpu.VMEM((lo, inner, kv, count), BF16),
            pltpu.VMEM((kv_heads, count, group * count), F32),
            pltpu.VMEM((inner, count, kv), F32),
            pltpu.VMEM((inner, count, kv), BF16),
            pltpu.VMEM((inner, count, kv), BF16),
            pltpu.VMEM((runs, kv, width), F32),
            pltpu.VMEM((Z_SPLIT, oc, kv), BF16),
            pltpu.VMEM((Z_SPLIT, oc, kv), BF16),
            dma((4,)),
            dma((lo, runs)),
            dma((inner, lo, runs)),
            dma((inner, lo, runs)),
            dma((lo, inner, runs)),
            dma((lo, inner, runs)),
            dma((inner,)),
            dma((inner,)),
            dma((lo, inner)),
            dma((lo, inner)),
            dma((inner,)),
            dma((inner,)),
            dma((Z_SPLIT,)),
            dma((Z_SPLIT,)),
        ],
        compiler_params=pltpu.CompilerParams(
            has_side_effects=True, vmem_limit_bytes=50 * 1024 * 1024),
        cost_estimate=pl.CostEstimate(
            flops=4 * 1024 * 1024 * 1024, bytes_accessed=16 * 1024 * 1024, transcendentals=1024 * 1024),
    )(layer_input, queries, key_states, output_grad, value_weight, value_scales.T)


def solution(mesh):
    both = P(("outer", "inner"), None)
    return jax.shard_map(
        on_device, mesh=mesh,
        in_specs=(both, both, both, both, P("inner", None), P("inner", None)),
        out_specs=(both, both, both), check_vma=False)
```

```python
import functools
import jax
import jax.numpy as jnp
from jax import lax
from jax.experimental import pallas as pl
from jax.experimental.pallas import tpu as pltpu
from jax.sharding import PartitionSpec as P

HEAD_DIM = 128
QUANT_BLOCK = 256
CLIP_RATIO = 1.5
Z_SPLIT = 4
F32 = jnp.float32
BF16 = jnp.bfloat16


def dot(a, b, ca=1, cb=0):
    return lax.dot_general(a, b, (((ca,), (cb,)), ((), ())), preferred_element_type=F32)


def body(dims, li, q_hbm, k_hbm, g_hbm, w_hbm, sc_ref, dq_hbm, dk_hbm, dw_out,
         q, k, g, w, xbuf, tbuf, vgbuf, probs, vals, vsend, vrecv, acc, pbuf, rbuf, dq_out, dk_out,
         loc_sem, own_sem, xs_sem, xr_sem, fs_sem, fr_sem, gxs_sem, gxr_sem, gfs_sem, gfr_sem,
         vs_sem, vr_sem, zs_sem, zr_sem, out_sem):
    outer, inner, lo, strips, sub, oc, kv_heads, group = dims
    o = lax.axis_index("outer")
    x = lax.axis_index("inner")
    z = o // lo
    l = o % lo
    pairs = lo // 2
    part = outer * oc
    runs = strips * sub
    per = Z_SPLIT // runs
    width = per * oc
    count = q.shape[0]
    scale = HEAD_DIM ** -0.5

    def peer(e):
        return ((l // 2 + e // 2) % pairs) * 2 + (l + e) % 2

    def back(e):
        return ((pairs - e // 2) % pairs) * 2 + e % 2

    def block_of(who, r):
        return (r // sub) * (outer // strips) + who * (Z_SPLIT // strips) + (r % sub) * per

    def col(e, r):
        return pl.multiple_of(block_of(peer(e), r) * oc, 128)

    def xdev(e):
        return (o, (x + e) % inner)

    def ldev(e):
        return (z * lo + peer(e), x)

    def remote(src, dst, ss, rs, dev):
        return pltpu.make_async_remote_copy(
            src_ref=src, dst_ref=dst, send_sem=ss, recv_sem=rs, device_id=dev,
            device_id_type=pl.DeviceIdType.MESH)

    q_cp = pltpu.make_async_copy(q_hbm, q, loc_sem.at[0])
    k_cp = pltpu.make_async_copy(k_hbm, k, loc_sem.at[1])
    g_cp = pltpu.make_async_copy(g_hbm, g, loc_sem.at[2])
    w_cp = pltpu.make_async_copy(w_hbm, w, loc_sem.at[3])
    order = list(range(2, lo)) + [1, 0]

    def x_copy(ex, e, r):
        cols = pl.multiple_of(((x + ex) % inner) * part + col(e, r), 128)
        return remote(li.at[:, pl.ds(cols, width)], xbuf.at[inner - ex, e, r],
                      xs_sem.at[ex, e, r], xr_sem.at[inner - ex, e, r], xdev(ex))

    def own_copy(e, r):
        cols = pl.multiple_of(x * part + col(e, r), 128)
        return pltpu.make_async_copy(li.at[:, pl.ds(cols, width)], xbuf.at[0, e, r], own_sem.at[e, r])

    def fwd_own(e, r):
        cols = pl.multiple_of(x * part + col(e, r), 128)
        return remote(li.at[:, pl.ds(cols, width)], tbuf.at[back(e), 0, r],
                      fs_sem.at[e, 0, r], fr_sem.at[back(e), 0, r], ldev(e))

    def fwd(s, e, r):
        return remote(xbuf.at[s, e, r], tbuf.at[back(e), s, r],
                      fs_sem.at[e, s, r], fr_sem.at[back(e), s, r], ldev(e))

    def issue(r):
        for e in order:
            for ex in range(1, inner):
                x_copy(ex, e, r).start()
            if e:
                fwd_own(e, r).start()

    k_cp.start()
    q_cp.start()
    issue(0)
    g_cp.start()
    for r in range(runs):
        for e in order:
            own_copy(e, r).start()
    w_cp.start()

    k_cp.wait()
    q_cp.wait()
    g_cp.wait()

    def heads(ref, h):
        return jnp.concatenate(
            [ref[:, (h * group + e) * HEAD_DIM:(h * group + e + 1) * HEAD_DIM] for e in range(group)], axis=0)

    key_pos = lax.broadcasted_iota(jnp.int32, (count, group * count), 0)
    query_pos = lax.broadcasted_iota(jnp.int32, (count, group * count), 1) % count
    admitted = key_pos <= query_pos
    for h in range(kv_heads):
        keys = k[:, h * HEAD_DIM:(h + 1) * HEAD_DIM]
        st = dot(keys, heads(q, h), 1, 1)
        st = jnp.where(admitted, st, -1e30)
        ex = jnp.exp((st - jnp.max(st, axis=0, keepdims=True)) * scale)
        p = ex * (1.0 / jnp.sum(ex, axis=0, keepdims=True))
        probs[h] = p
        vg = dot(p.astype(BF16), heads(g, h))
        vgbuf[0, 0, h * HEAD_DIM:(h + 1) * HEAD_DIM, :] = vg.T.astype(BF16)

    def vg_x(ex):
        return remote(vgbuf.at[0, 0], vgbuf.at[0, inner - ex], gxs_sem.at[ex], gxr_sem.at[inner - ex], xdev(ex))

    def vg_y(e, s):
        return remote(vgbuf.at[0, s], vgbuf.at[back(e), s], gfs_sem.at[e, s], gfr_sem.at[back(e), s], ldev(e))

    def vg_c(e, s):
        return remote(vgbuf.at[e, s], vgbuf.at[e + 1, s], gfs_sem.at[e + 1, s], gfr_sem.at[e + 1, s], ldev(1))

    chips = list(range(2, lo, 2))

    def share_vg(s):
        for e in chips:
            vg_y(e, s).start()
        vg_c(0, s).start()

    for ex in range(1, inner):
        vg_x(ex).start()
    share_vg(0)

    tile = min(width, 256)

    def add_term(vg_of, data_of, r, fresh):
        def step(c, carry):
            at = pl.multiple_of(c * tile, 128)
            data = data_of(at)
            for j in range(acc.shape[1] // QUANT_BLOCK):
                rows = slice(j * QUANT_BLOCK, (j + 1) * QUANT_BLOCK)
                term = dot(vg_of(rows), data)
                mean = jnp.sum(term * term, axis=0, keepdims=True) * (1.0 / QUANT_BLOCK)
                bound = CLIP_RATIO * jnp.sqrt(mean + 1e-6)
                kept = jnp.minimum(jnp.maximum(term, -bound), bound)
                if fresh:
                    acc[r, rows, pl.ds(at, tile)] = kept
                else:
                    acc[r, rows, pl.ds(at, tile)] += kept
            return carry
        lax.fori_loop(0, width // tile, step, 0)

    def terms(d, r):
        if d == 0:
            for s in range(inner):
                add_term(lambda rows, s=s: vgbuf[0, s, rows, :],
                         lambda at, s=s: xbuf[s, 0, r, :, pl.ds(at, tile)], r, s == 0)
            return

        for s in range(inner):
            arrived = pltpu.make_async_copy(tbuf.at[d, s, r], tbuf.at[d, s, r], fr_sem.at[d, s, r])
            arrived.wait()

        def one(s, carry):
            add_term(lambda rows: vgbuf[d, s, rows, :],
                     lambda at: tbuf[d, s, r, :, pl.ds(at, tile)], r, False)
            return carry
        lax.fori_loop(0, inner, one, 0)

    def owner(r, j):
        index = x * outer + block_of(l, r) + j
        return index // inner, index % inner

    def z_copy(r, j):
        oo, xx = owner(r, j)
        n = r * per + j
        return remote(pbuf.at[n], rbuf.at[z], zs_sem.at[n], zr_sem.at[z], (oo, xx))

    def is_me(r, j):
        oo, xx = owner(r, j)
        return jnp.logical_and(oo == o, xx == x)

    def deliver(r):
        summed = acc[r].T.astype(BF16)
        for j in range(per):
            n = r * per + j
            pbuf[n] = summed[j * oc:(j + 1) * oc]

            @pl.when(jnp.logical_not(is_me(r, j)))
            def _():
                z_copy(r, j).start()

            @pl.when(is_me(r, j))
            def _():
                pltpu.make_async_copy(pbuf.at[n], rbuf.at[z], zr_sem.at[z]).start()

    def val_copy(ex):
        return remote(vsend.at[ex], vrecv.at[inner - ex], vs_sem.at[ex], vr_sem.at[inner - ex], xdev(ex))

    def vg_arrived(e, s):
        pltpu.make_async_copy(vgbuf.at[e, s], vgbuf.at[e, s], gfr_sem.at[e, s]).wait()

    w_cp.wait()
    forward_order = [0] + list(range(1, lo))
    for r in range(runs):
        if r + 1 < runs:
            issue(r + 1)
        if r == 1 or runs == 1:
            for s in range(inner):
                for e in chips:
                    vg_arrived(e, s)
                    vg_c(e, s).start()
            for s in range(inner):
                for e in range(1, lo, 2):
                    vg_arrived(e, s)
        for i, e in enumerate(order):
            own_copy(e, r).wait()
            for s in range(1, inner):
                x_copy(inner - s, e, r).wait_recv()
                if e:
                    fwd(s, e, r).start()
            if r == 0 and i == 1:
                for s in range(1, inner):
                    vg_x(inner - s).wait_recv()
                    share_vg(s)
            start = col(e, r)
            for j in range(vals.shape[-1] // QUANT_BLOCK):
                block = slice(j * QUANT_BLOCK, (j + 1) * QUANT_BLOCK)
                row_scale = sc_ref[j:j + 1, pl.ds(start, width)]
                lhs = jnp.concatenate(
                    [(xbuf[s, e, r].astype(F32) * row_scale).astype(BF16) for s in range(inner)], axis=0)
                add = dot(lhs, w[pl.ds(start, width), block]).reshape(inner, count, QUANT_BLOCK)
                if r == 0 and i == 0:
                    vals[:, :, block] = add
                else:
                    vals[:, :, block] += add
            if r:
                terms(forward_order[i], r - 1)
        if r:
            deliver(r - 1)

    for ex in range(1, inner):
        vsend[ex] = vals[ex].astype(BF16)
        val_copy(ex).start()
    for d in forward_order:
        terms(d, runs - 1)
    deliver(runs - 1)

    for s in range(1, inner):
        val_copy(inner - s).wait_recv()
    total = vals[0]
    for s in range(1, inner):
        total = total + vrecv[s].astype(F32)
    values = total.astype(BF16)
    for h in range(kv_heads):
        cols = slice(h * HEAD_DIM, (h + 1) * HEAD_DIM)
        keys = k[:, cols]
        dp = dot(values[:, cols], heads(g, h), 1, 1)
        p = probs[h]
        delta = jnp.sum(p * dp, axis=0, keepdims=True)
        ds = p * (dp - delta)
        dk_out[:, cols] = (dot(ds.astype(BF16), heads(q, h)) * scale).astype(BF16)
        dq = (dot(ds.T.astype(BF16), keys) * scale).astype(BF16)
        for e in range(group):
            dq_out[:, (h * group + e) * HEAD_DIM:(h * group + e + 1) * HEAD_DIM] = dq[e * count:(e + 1) * count]
    dq_cp = pltpu.make_async_copy(dq_out, dq_hbm, out_sem.at[0])
    dk_cp = pltpu.make_async_copy(dk_out, dk_hbm, out_sem.at[1])
    dq_cp.start()
    dk_cp.start()

    for ex in range(1, inner):
        vg_x(ex).wait_send()
        val_copy(ex).wait_send()
        for r in range(runs):
            for e in order:
                x_copy(ex, e, r).wait_send()
    for s in range(inner):
        vg_c(0, s).wait_send()
        for e in chips:
            vg_y(e, s).wait_send()
            vg_c(e, s).wait_send()
        for e in range(1, lo):
            for r in range(runs):
                (fwd(s, e, r) if s else fwd_own(e, r)).wait_send()

    for n in range(Z_SPLIT):
        pltpu.make_async_copy(rbuf.at[n], rbuf.at[n], zr_sem.at[n]).wait()
    out = rbuf[0].astype(F32)
    for n in range(1, Z_SPLIT):
        out = out + rbuf[n].astype(F32)
    dw_out[...] = out
    for r in range(runs):
        for j in range(per):
            @pl.when(jnp.logical_not(is_me(r, j)))
            def _():
                z_copy(r, j).wait_send()
    dq_cp.wait()
    dk_cp.wait()


def on_device(layer_input, queries, key_states, output_grad, value_weight, value_scales):
    outer = lax.axis_size("outer")
    inner = lax.axis_size("inner")
    lo = outer // Z_SPLIT
    count, model = layer_input.shape
    kv = key_states.shape[1]
    oc = model // (outer * inner)
    strips = 2 if (2 * oc) % 128 == 0 else 1
    sub = 2 if oc % 128 == 0 else 1
    runs = strips * sub
    per = Z_SPLIT // runs
    width = per * oc
    kv_heads = kv // HEAD_DIM
    group = queries.shape[1] // kv
    dims = (outer, inner, lo, strips, sub, oc, kv_heads, group)
    dma = pltpu.SemaphoreType.DMA
    anyspace = pl.BlockSpec(memory_space=pl.ANY)
    vmem = pl.BlockSpec(memory_space=pltpu.VMEM)
    return pl.pallas_call(
        functools.partial(body, dims),
        out_shape=(
            jax.ShapeDtypeStruct(queries.shape, BF16),
            jax.ShapeDtypeStruct(key_states.shape, BF16),
            jax.ShapeDtypeStruct((oc, kv), F32),
        ),
        in_specs=[anyspace] * 5 + [vmem],
        out_specs=(anyspace, anyspace, vmem),
        scratch_shapes=[
            pltpu.VMEM(queries.shape, BF16),
            pltpu.VMEM(key_states.shape, BF16),
            pltpu.VMEM(output_grad.shape, BF16),
            pltpu.VMEM(value_weight.shape, BF16),
            pltpu.VMEM((inner, lo, runs, count, width), BF16),
            pltpu.VMEM((lo, inner, runs, count, width), BF16),
            pltpu.VMEM((lo, inner, kv, count), BF16),
            pltpu.VMEM((kv_heads, count, group * count), F32),
            pltpu.VMEM((inner, count, kv), F32),
            pltpu.VMEM((inner, count, kv), BF16),
            pltpu.VMEM((inner, count, kv), BF16),
            pltpu.VMEM((runs, kv, width), F32),
            pltpu.VMEM((Z_SPLIT, oc, kv), BF16),
            pltpu.VMEM((Z_SPLIT, oc, kv), BF16),
            pltpu.VMEM(queries.shape, BF16),
            pltpu.VMEM(key_states.shape, BF16),
            dma((4,)),
            dma((lo, runs)),
            dma((inner, lo, runs)),
            dma((inner, lo, runs)),
            dma((lo, inner, runs)),
            dma((lo, inner, runs)),
            dma((inner,)),
            dma((inner,)),
            dma((lo, inner)),
            dma((lo, inner)),
            dma((inner,)),
            dma((inner,)),
            dma((Z_SPLIT,)),
            dma((Z_SPLIT,)),
            dma((2,)),
        ],
        compiler_params=pltpu.CompilerParams(
            has_side_effects=True, vmem_limit_bytes=60 * 1024 * 1024),
        cost_estimate=pl.CostEstimate(
            flops=4 * 1024 * 1024 * 1024, bytes_accessed=16 * 1024 * 1024, transcendentals=1024 * 1024),
    )(layer_input, queries, key_states, output_grad, value_weight, value_scales.T)


def solution(mesh):
    both = P(("outer", "inner"), None)
    return jax.shard_map(
        on_device, mesh=mesh,
        in_specs=(both, both, both, both, P("inner", None), P("inner", None)),
        out_specs=(both, both, both), check_vma=False)
```

```python
import functools
import jax
import jax.numpy as jnp
from jax import lax
from jax.experimental import pallas as pl
from jax.experimental.pallas import tpu as pltpu
from jax.sharding import PartitionSpec as P

HEAD_DIM = 128
QUANT_BLOCK = 256
CLIP_RATIO = 1.5
Z_SPLIT = 4
F32 = jnp.float32
BF16 = jnp.bfloat16


def dot(a, b, ca=1, cb=0):
    return lax.dot_general(a, b, (((ca,), (cb,)), ((), ())), preferred_element_type=F32)


def body(dims, li, q_hbm, k_hbm, g_hbm, w_hbm, sc_ref, dq_hbm, dk_hbm, dw_out,
         q, k, g, w, xbuf, tbuf, vgbuf, probs, vals, vsend, vrecv, acc, pbuf, rbuf, dq_out, dk_out,
         loc_sem, own_sem, xs_sem, xr_sem, fs_sem, fr_sem, gxs_sem, gxr_sem, gfs_sem, gfr_sem,
         vs_sem, vr_sem, zs_sem, zr_sem, out_sem, hops, hr_sem, hs_sem):
    outer, inner, lo, strips, sub, oc, kv_heads, group = dims
    o = lax.axis_index("outer")
    x = lax.axis_index("inner")
    z = o // lo
    l = o % lo
    pairs = lo // 2
    part = outer * oc
    runs = strips * sub
    per = Z_SPLIT // runs
    width = per * oc
    count = q.shape[0]
    scale = HEAD_DIM ** -0.5
    hop = inner == 2 and sub == 2

    def peer(e):
        return ((l // 2 + e // 2) % pairs) * 2 + (l + e) % 2

    def back(e):
        return ((pairs - e // 2) % pairs) * 2 + e % 2

    def block_of(who, r, at):
        low = (r % sub + 1 + at) % 2 if hop else r % sub
        strip = r // sub
        strip = strip + (at // (inner // 2)) * (strips - 1 - 2 * strip)
        return strip * (outer // strips) + who * (Z_SPLIT // strips) + low * per

    def col(e, r, at):
        return pl.multiple_of(block_of(peer(e), r, at) * oc, 128)

    def xdev(e):
        return (o, (x + e) % inner)

    def ldev(e):
        return (z * lo + peer(e), x)

    def remote(src, dst, ss, rs, dev):
        return pltpu.make_async_remote_copy(
            src_ref=src, dst_ref=dst, send_sem=ss, recv_sem=rs, device_id=dev,
            device_id_type=pl.DeviceIdType.MESH)

    q_cp = pltpu.make_async_copy(q_hbm, q, loc_sem.at[0])
    k_cp = pltpu.make_async_copy(k_hbm, k, loc_sem.at[1])
    g_cp = pltpu.make_async_copy(g_hbm, g, loc_sem.at[2])
    w_cp = pltpu.make_async_copy(w_hbm, w, loc_sem.at[3])
    order = list(range(2, lo)) + [1, 0]

    def x_copy(ex, e, r):
        to = (x + ex) % inner
        cols = pl.multiple_of(to * part + col(e, r, to), 128)
        return remote(li.at[:, pl.ds(cols, width)], xbuf.at[inner - ex, e, r],
                      xs_sem.at[ex, e, r], xr_sem.at[inner - ex, e, r], xdev(ex))

    def own_copy(e, r):
        cols = pl.multiple_of(x * part + col(e, r, x), 128)
        return pltpu.make_async_copy(li.at[:, pl.ds(cols, width)], xbuf.at[0, e, r], own_sem.at[e, r])

    def fwd_own(e, r):
        cols = pl.multiple_of(x * part + col(e, r, x), 128)
        return remote(li.at[:, pl.ds(cols, width)], tbuf.at[back(e), 0, r],
                      fs_sem.at[e, 0, r], fr_sem.at[back(e), 0, r], ldev(e))

    def fwd(s, e, r):
        return remote(xbuf.at[s, e, r], tbuf.at[back(e), s, r],
                      fs_sem.at[e, s, r], fr_sem.at[back(e), s, r], ldev(e))

    def issue(r):
        for e in order:
            for ex in range(1, inner):
                x_copy(ex, e, r).start()
            if e:
                fwd_own(e, r).start()

    k_cp.start()
    q_cp.start()
    issue(0)
    g_cp.start()
    for r in range(runs):
        for e in order:
            own_copy(e, r).start()
    w_cp.start()

    k_cp.wait()
    q_cp.wait()
    g_cp.wait()

    def heads(ref, h):
        return jnp.concatenate(
            [ref[:, (h * group + e) * HEAD_DIM:(h * group + e + 1) * HEAD_DIM] for e in range(group)], axis=0)

    key_pos = lax.broadcasted_iota(jnp.int32, (count, group * count), 0)
    query_pos = lax.broadcasted_iota(jnp.int32, (count, group * count), 1) % count
    admitted = key_pos <= query_pos
    for h in range(kv_heads):
        keys = k[:, h * HEAD_DIM:(h + 1) * HEAD_DIM]
        st = dot(keys, heads(q, h), 1, 1)
        st = jnp.where(admitted, st, -1e30)
        ex = jnp.exp((st - jnp.max(st, axis=0, keepdims=True)) * scale)
        p = ex * (1.0 / jnp.sum(ex, axis=0, keepdims=True))
        probs[h] = p
        vg = dot(p.astype(BF16), heads(g, h))
        vgbuf[0, 0, h * HEAD_DIM:(h + 1) * HEAD_DIM, :] = vg.T.astype(BF16)

    def vg_x(ex):
        return remote(vgbuf.at[0, 0], vgbuf.at[0, inner - ex], gxs_sem.at[ex], gxr_sem.at[inner - ex], xdev(ex))

    def vg_y(e, s):
        return remote(vgbuf.at[0, s], vgbuf.at[back(e), s], gfs_sem.at[e, s], gfr_sem.at[back(e), s], ldev(e))

    def vg_c(e, s):
        return remote(vgbuf.at[e, s], vgbuf.at[e + 1, s], gfs_sem.at[e + 1, s], gfr_sem.at[e + 1, s], ldev(1))

    chips = list(range(2, lo, 2))

    def share_vg(s):
        for e in chips:
            vg_y(e, s).start()
        vg_c(0, s).start()

    for ex in range(1, inner):
        vg_x(ex).start()
    share_vg(0)

    tile = min(width, 256)

    def add_term(vg_of, data_of, r, fresh):
        def step(c, carry):
            at = pl.multiple_of(c * tile, 128)
            data = data_of(at)
            for j in range(acc.shape[1] // QUANT_BLOCK):
                rows = slice(j * QUANT_BLOCK, (j + 1) * QUANT_BLOCK)
                term = dot(vg_of(rows), data)
                mean = jnp.sum(term * term, axis=0, keepdims=True) * (1.0 / QUANT_BLOCK)
                bound = CLIP_RATIO * jnp.sqrt(mean + 1e-6)
                kept = jnp.minimum(jnp.maximum(term, -bound), bound)
                if fresh:
                    acc[r, rows, pl.ds(at, tile)] = kept
                else:
                    acc[r, rows, pl.ds(at, tile)] += kept
            return carry
        lax.fori_loop(0, width // tile, step, 0)

    def terms(d, r):
        if d == 0:
            for s in range(inner):
                add_term(lambda rows, s=s: vgbuf[0, s, rows, :],
                         lambda at, s=s: xbuf[s, 0, r, :, pl.ds(at, tile)], r, s == 0)
            return

        for s in range(inner):
            arrived = pltpu.make_async_copy(tbuf.at[d, s, r], tbuf.at[d, s, r], fr_sem.at[d, s, r])
            arrived.wait()

        def one(s, carry):
            add_term(lambda rows: vgbuf[d, s, rows, :],
                     lambda at: tbuf[d, s, r, :, pl.ds(at, tile)], r, False)
            return carry
        lax.fori_loop(0, inner, one, 0)

    def owner(r, j):
        index = x * outer + block_of(l, r, x) + j
        return index // inner, index % inner

    def z_copy(r, j):
        oo, xx = owner(r, j)
        n = r * per + j
        return remote(pbuf.at[n], rbuf.at[z], zs_sem.at[n], zr_sem.at[z], (oo, xx))

    def is_me(r, j):
        oo, xx = owner(r, j)
        return jnp.logical_and(oo == o, xx == x)

    def cross(r):
        return remote(pbuf.at[r], hops.at[r // 2], zs_sem.at[r], hr_sem.at[r // 2], xdev(1))

    def onward(r):
        oo = ((1 - x) * outer + block_of(l, r, 1 - x)) // inner
        return oo, remote(hops.at[r // 2], rbuf.at[z], hs_sem.at[r // 2], zr_sem.at[z], (oo, x))

    def pass_on(r):
        cross(r).wait_recv()
        oo, copy = onward(r)

        @pl.when(oo != o)
        def _():
            copy.start()

        @pl.when(oo == o)
        def _():
            pltpu.make_async_copy(hops.at[r // 2], rbuf.at[z], zr_sem.at[z]).start()

    def deliver(r):
        summed = acc[r].T.astype(BF16)
        for j in range(per):
            n = r * per + j
            pbuf[n] = summed[j * oc:(j + 1) * oc]
            if hop and r % 2 == 0:
                cross(r).start()
                continue

            @pl.when(jnp.logical_not(is_me(r, j)))
            def _():
                z_copy(r, j).start()

            @pl.when(is_me(r, j))
            def _():
                pltpu.make_async_copy(pbuf.at[n], rbuf.at[z], zr_sem.at[z]).start()
        if hop and r % 2 == 1:
            pass_on(r - 1)

    def val_copy(ex):
        return remote(vsend.at[ex], vrecv.at[inner - ex], vs_sem.at[ex], vr_sem.at[inner - ex], xdev(ex))

    def vg_arrived(e, s):
        pltpu.make_async_copy(vgbuf.at[e, s], vgbuf.at[e, s], gfr_sem.at[e, s]).wait()

    w_cp.wait()
    forward_order = [0] + list(range(1, lo))
    for r in range(runs):
        if r + 1 < runs:
            issue(r + 1)
        if r == 1 or runs == 1:
            for s in range(inner):
                for e in chips:
                    vg_arrived(e, s)
                    vg_c(e, s).start()
            for s in range(inner):
                for e in range(1, lo, 2):
                    vg_arrived(e, s)
        for i, e in enumerate(order):
            own_copy(e, r).wait()
            for s in range(1, inner):
                x_copy(inner - s, e, r).wait_recv()
                if e:
                    fwd(s, e, r).start()
            if r == 0 and i == 1:
                for s in range(1, inner):
                    vg_x(inner - s).wait_recv()
                    share_vg(s)
            start = col(e, r, x)
            for j in range(vals.shape[-1] // QUANT_BLOCK):
                block = slice(j * QUANT_BLOCK, (j + 1) * QUANT_BLOCK)
                row_scale = sc_ref[j:j + 1, pl.ds(start, width)]
                lhs = jnp.concatenate(
                    [(xbuf[s, e, r].astype(F32) * row_scale).astype(BF16) for s in range(inner)], axis=0)
                add = dot(lhs, w[pl.ds(start, width), block]).reshape(inner, count, QUANT_BLOCK)
                if r == 0 and i == 0:
                    vals[:, :, block] = add
                else:
                    vals[:, :, block] += add
            if r:
                terms(forward_order[i], r - 1)
        if r:
            deliver(r - 1)

    for ex in range(1, inner):
        vsend[ex] = vals[ex].astype(BF16)
        val_copy(ex).start()
    for d in forward_order:
        terms(d, runs - 1)
    deliver(runs - 1)

    for s in range(1, inner):
        val_copy(inner - s).wait_recv()
    total = vals[0]
    for s in range(1, inner):
        total = total + vrecv[s].astype(F32)
    values = total.astype(BF16)
    for h in range(kv_heads):
        cols = slice(h * HEAD_DIM, (h + 1) * HEAD_DIM)
        keys = k[:, cols]
        dp = dot(values[:, cols], heads(g, h), 1, 1)
        p = probs[h]
        delta = jnp.sum(p * dp, axis=0, keepdims=True)
        ds = p * (dp - delta)
        dk_out[:, cols] = (dot(ds.astype(BF16), heads(q, h)) * scale).astype(BF16)
        dq = (dot(ds.T.astype(BF16), keys) * scale).astype(BF16)
        for e in range(group):
            dq_out[:, (h * group + e) * HEAD_DIM:(h * group + e + 1) * HEAD_DIM] = dq[e * count:(e + 1) * count]
    dq_cp = pltpu.make_async_copy(dq_out, dq_hbm, out_sem.at[0])
    dk_cp = pltpu.make_async_copy(dk_out, dk_hbm, out_sem.at[1])
    dq_cp.start()
    dk_cp.start()

    for ex in range(1, inner):
        vg_x(ex).wait_send()
        val_copy(ex).wait_send()
        for r in range(runs):
            for e in order:
                x_copy(ex, e, r).wait_send()
    for s in range(inner):
        vg_c(0, s).wait_send()
        for e in chips:
            vg_y(e, s).wait_send()
            vg_c(e, s).wait_send()
        for e in range(1, lo):
            for r in range(runs):
                (fwd(s, e, r) if s else fwd_own(e, r)).wait_send()

    for n in range(Z_SPLIT):
        pltpu.make_async_copy(rbuf.at[n], rbuf.at[n], zr_sem.at[n]).wait()
    out = rbuf[0].astype(F32)
    for n in range(1, Z_SPLIT):
        out = out + rbuf[n].astype(F32)
    dw_out[...] = out
    for r in range(runs):
        if hop and r % 2 == 0:
            cross(r).wait_send()
            oo, copy = onward(r)

            @pl.when(oo != o)
            def _():
                copy.wait_send()
            continue
        for j in range(per):
            @pl.when(jnp.logical_not(is_me(r, j)))
            def _():
                z_copy(r, j).wait_send()
    dq_cp.wait()
    dk_cp.wait()


def on_device(layer_input, queries, key_states, output_grad, value_weight, value_scales):
    outer = lax.axis_size("outer")
    inner = lax.axis_size("inner")
    lo = outer // Z_SPLIT
    count, model = layer_input.shape
    kv = key_states.shape[1]
    oc = model // (outer * inner)
    strips = 2 if (2 * oc) % 128 == 0 else 1
    sub = 2 if oc % 128 == 0 else 1
    runs = strips * sub
    per = Z_SPLIT // runs
    width = per * oc
    kv_heads = kv // HEAD_DIM
    group = queries.shape[1] // kv
    dims = (outer, inner, lo, strips, sub, oc, kv_heads, group)
    dma = pltpu.SemaphoreType.DMA
    anyspace = pl.BlockSpec(memory_space=pl.ANY)
    vmem = pl.BlockSpec(memory_space=pltpu.VMEM)
    return pl.pallas_call(
        functools.partial(body, dims),
        out_shape=(
            jax.ShapeDtypeStruct(queries.shape, BF16),
            jax.ShapeDtypeStruct(key_states.shape, BF16),
            jax.ShapeDtypeStruct((oc, kv), F32),
        ),
        in_specs=[anyspace] * 5 + [vmem],
        out_specs=(anyspace, anyspace, vmem),
        scratch_shapes=[
            pltpu.VMEM(queries.shape, BF16),
            pltpu.VMEM(key_states.shape, BF16),
            pltpu.VMEM(output_grad.shape, BF16),
            pltpu.VMEM(value_weight.shape, BF16),
            pltpu.VMEM((inner, lo, runs, count, width), BF16),
            pltpu.VMEM((lo, inner, runs, count, width), BF16),
            pltpu.VMEM((lo, inner, kv, count), BF16),
            pltpu.VMEM((kv_heads, count, group * count), F32),
            pltpu.VMEM((inner, count, kv), F32),
            pltpu.VMEM((inner, count, kv), BF16),
            pltpu.VMEM((inner, count, kv), BF16),
            pltpu.VMEM((runs, kv, width), F32),
            pltpu.VMEM((Z_SPLIT, oc, kv), BF16),
            pltpu.VMEM((Z_SPLIT, oc, kv), BF16),
            pltpu.VMEM(queries.shape, BF16),
            pltpu.VMEM(key_states.shape, BF16),
            dma((4,)),
            dma((lo, runs)),
            dma((inner, lo, runs)),
            dma((inner, lo, runs)),
            dma((lo, inner, runs)),
            dma((lo, inner, runs)),
            dma((inner,)),
            dma((inner,)),
            dma((lo, inner)),
            dma((lo, inner)),
            dma((inner,)),
            dma((inner,)),
            dma((Z_SPLIT,)),
            dma((Z_SPLIT,)),
            dma((2,)),
            pltpu.VMEM((2, oc, kv), BF16),
            dma((2,)),
            dma((2,)),
        ],
        compiler_params=pltpu.CompilerParams(
            has_side_effects=True, vmem_limit_bytes=60 * 1024 * 1024),
        cost_estimate=pl.CostEstimate(
            flops=4 * 1024 * 1024 * 1024, bytes_accessed=16 * 1024 * 1024, transcendentals=1024 * 1024),
    )(layer_input, queries, key_states, output_grad, value_weight, value_scales.T)


def solution(mesh):
    both = P(("outer", "inner"), None)
    return jax.shard_map(
        on_device, mesh=mesh,
        in_specs=(both, both, both, both, P("inner", None), P("inner", None)),
        out_specs=(both, both, both), check_vma=False)
```
